512 devices in a mesh: seq: 64 (over z, x, core), tp: 8 (over y).
Axes of the slice: x: 4, y: 8, z: 8, core: 2. Of those that a mesh axis runs over, the one named last changes fastest.
Arguments:
- query: bfloat16 [8192, 8192], P('seq', 'tp'), may hold values from -1024 to 1024
- vision_kv: bfloat16 [2048, 2048], P(('seq', 'tp')), may hold values from -512 to 512
- key_gain: float32 [128], replicated, may hold values from 0.1 to 1.9
- out_grad: bfloat16 [8192, 8192], P('seq', 'tp'), may hold values from -4 to 4
- span_image: int32 [128], replicated, may hold values from 0 to 1, as said below
- span_tiles: int32 [128], replicated, may hold values from 0 to 4, as said below
Outputs:
- attn_out: bfloat16 [8192, 8192], P('seq', 'tp')
- query_grad: bfloat16 [8192, 8192], P('seq', 'tp')
- kv_grad: bfloat16 [2048, 2048], P(('seq', 'tp'))
The draws below stay inside these ranges and needn't reach their ends.
Inputs may be any that keep to these rules, and one draw needn't show every extreme that they name: span_image never falls from one block to the next; the blocks from some block in the second half of the text on see image 1. span_tiles is zero exactly on the leading blocks before the first block that sees an image (block 0 always among them); the first block that sees each image sees all 4 of its tiles.
All inputs are finite; a program needn't handle non-finite values.
Results may differ from the reference program's by a relative error of at most 0.013.
Values may be sent and summed in bfloat16 or wider, within the bound.
No kernel may reach another device: no remote copies, remote signals or barrier semaphores. Data moves between devices by JAX's collectives and lax.ppermute only.
A program may use at most 64 MiB of HBM per device.

```python
import math
import jax
import jax.numpy as jnp
from jax import lax

HQ = 64
KVH = 8
HD = 128
BLOCK = 64
TILES_IMG = 4
TOKENS = 8192
VIS = 2048
TILE_TOK = 256
BLOCKS = 128


def span_layout(key):
    key = jax.random.fold_in(key, 11)
    key_first, key_second, key_counts = jax.random.split(key, 3)
    quarter = max(BLOCKS // 4, 1)
    first_block = jax.random.randint(key_first, (), 1, quarter + 1)
    second_block = jax.random.randint(key_second, (), BLOCKS // 2, BLOCKS // 2 + quarter)
    return (first_block, second_block, key_counts)


def vision_rows(key, spread):
    key = jax.random.fold_in(key, 17)
    key_rows, key_cols, key_base = jax.random.split(key, 3)
    row_scale = jnp.exp(jax.random.uniform(key_rows, (VIS, KVH, 1), jnp.float32) * math.log(spread))
    col_scale = jnp.exp(jax.random.uniform(key_cols, (1, KVH, HD), jnp.float32, -1.0, 1.0) * (0.5 * math.log(10.0)))
    base = jnp.clip(jax.random.normal(key_base, (VIS, KVH, HD), jnp.float32), -4.0, 4.0)
    position = jnp.arange(VIS)[:, None, None]
    near_rows = (position >= 8) & (position < 16)
    base = jnp.where(near_rows, base, base)
    return (row_scale, col_scale, base)


def draw_vision_kv(key, part):
    row_scale, col_scale, base = vision_rows(key, 10.0)
    key = jax.random.fold_in(key, 23)
    values = jnp.clip(jax.random.normal(key, (VIS, KVH, HD), jnp.float32), -4.0, 4.0)
    keys_part = row_scale * col_scale * base
    return jnp.stack([keys_part, values], axis=2).reshape(VIS, KVH * 2 * HD).astype(jnp.bfloat16)


def draw_query(key, part):
    key = jax.random.fold_in(key, 29)
    drawn = jnp.clip(2.5 * jax.random.normal(key, (TOKENS, HQ, HD), jnp.float32), -15.0, 15.0)
    return drawn.reshape(TOKENS, HQ * HD).astype(jnp.bfloat16)


def draw_span_image(key, part):
    first_block, second_block, unused = span_layout(key)
    return (jnp.arange(BLOCKS) >= second_block).astype(jnp.int32)


def draw_span_tiles(key, part):
    first_block, second_block, key_counts = span_layout(key)
    blocks = jnp.arange(BLOCKS)
    counts = jax.random.randint(key_counts, (BLOCKS,), 1, TILES_IMG + 1)
    counts = jnp.where(blocks < first_block, 0, counts)
    counts = jnp.where((blocks == first_block) | (blocks == second_block), TILES_IMG, counts)
    return counts.astype(jnp.int32)


def block_levels(rng, extent, cuts, smallest, high):
    def one(dim, shards_of):
        steps = jax.random.uniform(jax.random.fold_in(jax.random.fold_in(rng, 6), dim), (shards_of,), jnp.float32, smallest / len(cuts), high / len(cuts))
        return jnp.repeat(jnp.exp(steps), extent[dim] // shards_of).reshape((-1,) + (1,) * (len(extent) - dim - 1))

    level = one(*cuts[0])
    for cut in cuts[1:]:
        level = level * one(*cut)
    return level


def scatter_about(own_key, dims, scale, reach, shards=(), kind=jnp.bfloat16):
    entries = jax.random.normal(own_key, dims, jnp.float32) * scale
    if len(shards) > 0:
        entries = block_levels(own_key, dims, shards, -0.22, 0.18) * entries
    return jnp.clip(entries, min=-reach, max=reach).astype(kind)


def setup_inputs(seed: int = 0) -> dict:
    key_list = jax.random.split(jax.random.key(seed), 7)
    query = draw_query(jax.random.fold_in(key_list[6], 71), 0)
    vision_kv = draw_vision_kv(jax.random.fold_in(key_list[6], 71), 0)
    key_gain = jnp.clip(1.0 + 0.18 * jax.random.normal(key_list[2], (HD,), jnp.float32), 0.1, 1.9)
    out_grad = scatter_about(key_list[3], (TOKENS, HQ * HD), 0.5, 4.0, ((0, 64), (1, 8)))
    span_image = draw_span_image(jax.random.fold_in(key_list[6], 71), 0)
    span_tiles = draw_span_tiles(jax.random.fold_in(key_list[6], 71), 0)
    return dict(query=query, vision_kv=vision_kv, key_gain=key_gain, out_grad=out_grad, span_image=span_image, span_tiles=span_tiles)


epsilon = 1e-05
neg_fill = -1e+30

def one_head(query_h, grad_h, keys_h, values_h, visible, live_rows):
    score_scale = 1.0 / math.sqrt(HD)
    scores = jnp.dot(query_h, keys_h.T, preferred_element_type=jnp.float32) * score_scale
    scores = jnp.where(visible, scores, neg_fill)
    row_max = lax.optimization_barrier(jnp.max(scores, axis=1, keepdims=True))
    row_sum = lax.optimization_barrier(jnp.sum(jnp.where(visible, jnp.exp(scores - row_max), 0.0), axis=1, keepdims=True))
    row_sum = jnp.where(live_rows[:, None], row_sum, 1.0)
    log_total = row_max + jnp.log(row_sum)
    weights = jnp.where(visible, jnp.exp(scores - log_total), 0.0)
    rounded = weights.astype(jnp.bfloat16)
    attn_out = jnp.dot(rounded, values_h, preferred_element_type=jnp.float32).astype(jnp.bfloat16)
    prob_grad = jnp.dot(grad_h, values_h.T, preferred_element_type=jnp.float32)
    row_delta = lax.optimization_barrier(jnp.sum(grad_h.astype(jnp.float32) * attn_out.astype(jnp.float32), axis=1, keepdims=True))
    dscore = (weights * (prob_grad - row_delta)).astype(jnp.bfloat16)
    query_grad = (jnp.dot(dscore, keys_h, preferred_element_type=jnp.float32) * score_scale).astype(jnp.bfloat16)
    value_grad = jnp.dot(rounded.T, grad_h, preferred_element_type=jnp.float32)
    key_grad = jnp.dot(dscore.T, query_h, preferred_element_type=jnp.float32) * score_scale
    return (attn_out, query_grad, key_grad, value_grad)

def reference(query, vision_kv, key_gain, out_grad, span_image, span_tiles):
    vis_total = vision_kv.shape[0]
    tok_total = query.shape[0]
    group_size = HQ // KVH
    halves = vision_kv.reshape(vis_total, KVH, 2, HD)
    key_pre = halves[:, :, 0, :].astype(jnp.float32)
    inverse = lax.rsqrt(lax.optimization_barrier(jnp.mean(key_pre * key_pre, axis=2, keepdims=True)) + epsilon)
    normed = key_pre * inverse
    keys = (normed * key_gain).astype(jnp.bfloat16)
    values = halves[:, :, 1, :]
    block_of = jnp.arange(tok_total, dtype=jnp.int32) // BLOCK
    first_tile = span_image[block_of] * TILES_IMG
    last_tile = first_tile + span_tiles[block_of]
    tile_of = jnp.arange(vis_total, dtype=jnp.int32) // TILE_TOK
    visible = (tile_of[None, :] >= first_tile[:, None]) & (tile_of[None, :] < last_tile[:, None])
    live_rows = span_tiles[block_of] > 0
    query_t = query.reshape(tok_total, KVH, group_size, HD).transpose(1, 2, 0, 3)
    grad_t = out_grad.reshape(tok_total, KVH, group_size, HD).transpose(1, 2, 0, 3)
    keys_t = keys.transpose(1, 0, 2)
    values_t = values.transpose(1, 0, 2)

    def per_kv_head(items):
        query_h, grad_h, keys_h, values_h = items

        def query_head(inner):
            return one_head(inner[0], inner[1], keys_h, values_h, visible, live_rows)
        attn_out, query_grad, key_grad, value_grad = lax.map(query_head, (query_h, grad_h))
        return (attn_out, query_grad, lax.optimization_barrier(jnp.sum(key_grad, axis=0)), lax.optimization_barrier(jnp.sum(value_grad, axis=0)))
    attn_out, query_grad, key_grad, value_grad = lax.map(per_kv_head, (query_t, grad_t, keys_t, values_t))
    attn_out = attn_out.transpose(2, 0, 1, 3).reshape(tok_total, HQ * HD)
    query_grad = query_grad.transpose(2, 0, 1, 3).reshape(tok_total, HQ * HD)
    key_grad = key_grad.transpose(1, 0, 2)
    value_grad = value_grad.transpose(1, 0, 2)
    scaled = key_grad * key_gain
    pre_grad = inverse * (scaled - normed * lax.optimization_barrier(jnp.mean(scaled * normed, axis=2, keepdims=True)))
    kv_grad = jnp.stack([pre_grad, value_grad], axis=2).reshape(vis_total, KVH * 2 * HD).astype(jnp.bfloat16)
    return (attn_out, query_grad, kv_grad)
```

```python
import functools
import math

import jax
import jax.numpy as jnp
from jax import lax
from jax.experimental import pallas as pl
from jax.experimental.pallas import tpu as pltpu
from jax.sharding import Mesh, PartitionSpec as P

HD = 128
BLOCK = 64
TILES_IMG = 4

epsilon = 1e-05
neg_fill = -1e30
score_scale = 1.0 / math.sqrt(HD)

NN = (((1,), (0,)), ((), ()))
NT = (((1,), (1,)), ((), ()))
TN = (((0,), (0,)), ((), ()))


def dot(a, b, dims):
    return lax.dot_general(a, b, dims, preferred_element_type=jnp.float32)


def attention_kernel(
    seq_index, image_ref, tiles_ref, gain_ref, query_ref, grad_ref, kv_ref,
    out_ref, query_grad_ref, terms_ref, keys_ref, values_ref, key_acc, value_acc,
):
    groups, group_rows, _ = kv_ref.shape
    image_rows = group_rows // 2
    part = image_rows // TILES_IMG
    span = groups * image_rows
    heads = query_ref.shape[1] // HD
    begin = seq_index() * 2
    image_a, image_b = image_ref[begin], image_ref[begin + 1]
    tiles_a, tiles_b = tiles_ref[begin], tiles_ref[begin + 1]
    column = lax.broadcasted_iota(jnp.int32, (1, span), 1)
    column_tile = lax.rem(lax.div(column, part), TILES_IMG)

    def image_slice(image):
        return pl.ds(pl.multiple_of(image * image_rows, image_rows), image_rows)

    def load_image(image):
        rows = image_slice(image)
        pre = kv_ref[:, rows, :HD].astype(jnp.float32).reshape(span, HD)
        inverse = lax.rsqrt(jnp.mean(pre * pre, axis=1, keepdims=True) + epsilon)
        keys_ref[...] = (pre * inverse * gain_ref[...]).astype(jnp.bfloat16)
        values_ref[...] = kv_ref[:, rows, HD:].reshape(span, HD)

    def stacked(ref, row, first, count):
        return jnp.concatenate(
            [ref[row : row + BLOCK, j * HD : (j + 1) * HD] for j in range(first, first + count)], axis=0
        )

    def unstack(ref, row, first, count, rows):
        for j in range(count):
            ref[row : row + BLOCK, (first + j) * HD : (first + j + 1) * HD] = rows[j * BLOCK : (j + 1) * BLOCK]

    per_chunk = 4

    def block_step(row, tiles, fresh):
        bias = jnp.where(column_tile < tiles, 0.0, neg_fill)
        live = (tiles > 0).astype(jnp.float32)
        for first in range(0, heads, per_chunk):
            query = stacked(query_ref, row, first, per_chunk)
            grad = stacked(grad_ref, row, first, per_chunk)
            scores = dot(query, keys_ref[...], NT) + bias
            row_max = jnp.max(scores, axis=1, keepdims=True)
            terms = jnp.exp((scores - row_max) * score_scale)
            inverse_sum = live / jnp.sum(terms, axis=1, keepdims=True)
            weights = terms * inverse_sum
            probs = weights.astype(jnp.bfloat16)
            out = dot(probs, values_ref[...], NN).astype(jnp.bfloat16)
            unstack(out_ref, row, first, per_chunk, out)
            delta = jnp.sum(grad.astype(jnp.float32) * out.astype(jnp.float32), axis=1, keepdims=True)
            prob_grad = dot(grad, values_ref[...], NT)
            dscore = (weights * (prob_grad - delta)).astype(jnp.bfloat16)
            query_grad = (dot(dscore, keys_ref[...], NN) * score_scale).astype(jnp.bfloat16)
            unstack(query_grad_ref, row, first, per_chunk, query_grad)
            value_term = dot(probs, grad, TN)
            key_term = dot(dscore, query, TN)
            if fresh and first == 0:
                value_acc[...] = value_term
                key_acc[...] = key_term
            else:
                value_acc[...] += value_term
                key_acc[...] += key_term

    def store_terms(image):
        rows = image_slice(image)
        terms_ref[:, rows, :HD] = (
            (key_acc[...] * score_scale).astype(jnp.bfloat16).reshape(groups, image_rows, HD)
        )
        terms_ref[:, rows, HD:] = value_acc[...].astype(jnp.bfloat16).reshape(groups, image_rows, HD)

    load_image(image_a)
    block_step(0, tiles_a, True)

    @pl.when(image_a == image_b)
    def _():
        terms_ref[:, image_slice(1 - image_a), :] = jnp.zeros((groups, image_rows, 2 * HD), jnp.bfloat16)

    @pl.when(image_a != image_b)
    def _():
        store_terms(image_a)
        load_image(image_b)
        value_acc[...] = jnp.zeros_like(value_acc)
        key_acc[...] = jnp.zeros_like(key_acc)

    block_step(BLOCK, tiles_b, False)
    store_terms(image_b)


def attention(seq_index, span_image, span_tiles, key_gain, query, out_grad, kv):
    groups, group_rows, _ = kv.shape
    span = groups * group_rows // 2
    vmem = pl.BlockSpec(memory_space=pltpu.VMEM)
    smem = pl.BlockSpec(memory_space=pltpu.SMEM)
    work = 6 * 2 * query.size * span
    return pl.pallas_call(
        functools.partial(attention_kernel, seq_index),
        out_shape=[
            jax.ShapeDtypeStruct(query.shape, jnp.bfloat16),
            jax.ShapeDtypeStruct(query.shape, jnp.bfloat16),
            jax.ShapeDtypeStruct(kv.shape, jnp.bfloat16),
        ],
        in_specs=[smem, smem, vmem, vmem, vmem, vmem],
        out_specs=[vmem, vmem, vmem],
        scratch_shapes=[
            pltpu.VMEM((span, HD), jnp.bfloat16),
            pltpu.VMEM((span, HD), jnp.bfloat16),
            pltpu.VMEM((span, HD), jnp.float32),
            pltpu.VMEM((span, HD), jnp.float32),
        ],
        compiler_params=pltpu.CompilerParams(vmem_limit_bytes=40 * 1024 * 1024),
        cost_estimate=pl.CostEstimate(flops=work, bytes_accessed=5 * 1024 * 1024, transcendentals=query.size * span // HD),
        name="attention",
    )(span_image, span_tiles, key_gain, query, out_grad, kv)


def spread(rows, axes, copies):
    return lax.all_to_all(
        lax.optimization_barrier(jnp.broadcast_to(rows, (copies,) + rows.shape)), axes, split_axis=0, concat_axis=0
    )


def body(query, vision_kv, key_gain, out_grad, span_image, span_tiles):
    z, x, cores, tp = (lax.axis_size(name) for name in ("z", "x", "c", "tp"))
    own_rows = vision_kv.shape[0]
    share_rows = own_rows * tp

    by_head = vision_kv.reshape(own_rows, tp, 2 * HD).transpose(1, 0, 2)
    copies = lax.optimization_barrier(jnp.broadcast_to(by_head, (z,) + by_head.shape))
    along_z = lax.all_to_all(
        copies.reshape(z * tp, own_rows, 2 * HD), ("z", "tp"), split_axis=0, concat_axis=0, tiled=True
    )
    column = along_z.reshape(z * share_rows, 2 * HD)
    plane = spread(column, "x", x)
    kv = spread(plane, "c", cores).reshape(cores * x, z * share_rows, 2 * HD)

    def seq_index():
        return (lax.axis_index("z") * x + lax.axis_index("x")) * cores + lax.axis_index("c")

    attn_out, query_grad, terms = attention(
        seq_index, span_image, span_tiles, key_gain.reshape(1, HD), query, out_grad, kv
    )

    def fold(terms, axis, parts):
        got = lax.all_to_all(
            terms.reshape((parts, -1) + terms.shape[1:]), axis, split_axis=0, concat_axis=0
        )
        return jnp.sum(got.astype(jnp.float32), axis=0).astype(jnp.bfloat16)

    terms = fold(terms, "c", cores)
    terms = fold(terms, "x", x)
    got = lax.all_to_all(
        terms.reshape(z * tp, own_rows, 2 * HD), ("z", "tp"), split_axis=0, concat_axis=0, tiled=True
    )
    shares = jnp.sum(got.reshape(z, tp, own_rows, 2, HD).astype(jnp.float32), axis=0)

    halves = by_head.reshape(tp, own_rows, 2, HD)
    key_pre = halves[:, :, 0].astype(jnp.float32)
    inverse = lax.rsqrt(jnp.mean(key_pre * key_pre, axis=2, keepdims=True) + epsilon)
    normed = key_pre * inverse
    scaled = shares[:, :, 0] * key_gain
    pre_grad = inverse * (scaled - normed * jnp.mean(scaled * normed, axis=2, keepdims=True))
    kv_grad = jnp.stack([pre_grad, shares[:, :, 1]], axis=2).astype(jnp.bfloat16)
    kv_grad = kv_grad.reshape(tp, own_rows, 2 * HD).transpose(1, 0, 2).reshape(own_rows, tp * 2 * HD)
    return (attn_out, query_grad, kv_grad)


def solution(mesh):
    fine = Mesh(mesh.devices.reshape(8, 4, 2, 8), ("z", "x", "c", "tp"))
    seq = ("z", "x", "c")
    in_specs = (P(seq, "tp"), P(seq + ("tp",), None), P(), P(seq, "tp"), P(), P())
    out_specs = (P(seq, "tp"), P(seq, "tp"), P(seq + ("tp",), None))
    return jax.shard_map(body, mesh=fine, in_specs=in_specs, out_specs=out_specs, check_vma=False)
```

```python
import functools
import math

import jax
import jax.numpy as jnp
from jax import lax
from jax.experimental import pallas as pl
from jax.experimental.pallas import tpu as pltpu
from jax.sharding import Mesh, PartitionSpec as P

HD = 128
BLOCK = 64
TILES_IMG = 4

epsilon = 1e-05
neg_fill = -1e30
score_scale = 1.0 / math.sqrt(HD)

NN = (((1,), (0,)), ((), ()))
NT = (((1,), (1,)), ((), ()))
TN = (((0,), (0,)), ((), ()))


def dot(a, b, dims):
    return lax.dot_general(a, b, dims, preferred_element_type=jnp.float32)


def attention_kernel(
    info_ref, query_ref, grad_ref, kv_ref, out_ref, query_grad_ref, terms_ref, keys_ref, values_ref, key_acc, value_acc,
):
    groups, group_rows, _ = kv_ref.shape
    image_rows = group_rows // 2
    part = image_rows // TILES_IMG
    span = groups * image_rows
    heads = query_ref.shape[1] // HD
    lane = lax.broadcasted_iota(jnp.int32, info_ref.shape, 1)
    images, tiles = (
        [jnp.sum(jnp.where(lane == k, info_ref[...], 0.0)).astype(jnp.int32) for k in pair] for pair in ((0, 1), (2, 3))
    )
    mixed = images[0] != images[1]
    slots = [0, mixed.astype(jnp.int32)]

    def image_slice(image):
        return pl.ds(pl.multiple_of(image * image_rows, image_rows), image_rows)

    def load_image(slot, image):
        rows = image_slice(image)
        keys_ref[slot] = kv_ref[:, rows, :HD].reshape(span, HD)
        values_ref[slot] = kv_ref[:, rows, HD:].reshape(span, HD)

    def stacked(ref, row, first, count):
        return jnp.concatenate(
            [ref[row : row + BLOCK, j * HD : (j + 1) * HD] for j in range(first, first + count)], axis=0
        )

    def unstack(ref, row, first, count, rows):
        for j in range(count):
            ref[row : row + BLOCK, (first + j) * HD : (first + j + 1) * HD] = rows[j * BLOCK : (j + 1) * BLOCK]

    per_chunk = 4
    column = lax.broadcasted_iota(jnp.int32, (1, span), 1)
    column_tile = lax.rem(lax.div(column, part), TILES_IMG)
    bias = [jnp.where(column_tile < n, 0.0, neg_fill) for n in tiles]
    live = [(n > 0).astype(jnp.float32) for n in tiles]

    def front(b, first):
        query = stacked(query_ref, b * BLOCK, first, per_chunk)
        grad = stacked(grad_ref, b * BLOCK, first, per_chunk)
        scores = dot(query, keys_ref[slots[b]], NT) + bias[b]
        prob_grad = dot(grad, values_ref[slots[b]], NT)
        return query, grad, scores, prob_grad

    def middle(b, first, query, grad, scores, prob_grad):
        row_max = jnp.max(scores, axis=1, keepdims=True)
        terms = jnp.exp((scores - row_max) * score_scale)
        inverse_sum = live[b] / jnp.sum(terms, axis=1, keepdims=True)
        weights = terms * inverse_sum
        probs = weights.astype(jnp.bfloat16)
        out = dot(probs, values_ref[slots[b]], NN).astype(jnp.bfloat16)
        unstack(out_ref, b * BLOCK, first, per_chunk, out)
        delta = jnp.sum(grad.astype(jnp.float32) * out.astype(jnp.float32), axis=1, keepdims=True)
        dscore = (weights * (prob_grad - delta)).astype(jnp.bfloat16)
        return probs, dscore

    def back(b, first, query, grad, probs, dscore):
        query_grad = (dot(dscore, keys_ref[slots[b]], NN) * score_scale).astype(jnp.bfloat16)
        unstack(query_grad_ref, b * BLOCK, first, per_chunk, query_grad)
        value_term = dot(probs, grad, TN)
        key_term = dot(dscore, query, TN)
        if b == 0 and first == 0:
            value_acc[0] = value_term
            key_acc[0] = key_term
        else:
            value_acc[slots[b]] += value_term
            key_acc[slots[b]] += key_term

    def store_terms(slot, image):
        rows = image_slice(image)
        terms_ref[:, rows, :HD] = (
            (key_acc[slot] * score_scale).astype(jnp.bfloat16).reshape(groups, image_rows, HD)
        )
        terms_ref[:, rows, HD:] = value_acc[slot].astype(jnp.bfloat16).reshape(groups, image_rows, HD)

    load_image(0, images[0])

    @pl.when(mixed)
    def _():
        load_image(1, images[1])
        value_acc[1] = jnp.zeros((span, HD), jnp.float32)
        key_acc[1] = jnp.zeros((span, HD), jnp.float32)

    chunks = [(b, first) for b in range(2) for first in range(0, heads, per_chunk)]
    held = None
    for chunk in chunks:
        query, grad, scores, prob_grad = front(*chunk)
        if held is not None:
            back(*held)
        probs, dscore = middle(*chunk, query, grad, scores, prob_grad)
        held = (*chunk, query, grad, probs, dscore)
    back(*held)
    store_terms(0, images[0])

    @pl.when(mixed)
    def _():
        store_terms(1, images[1])

    @pl.when(jnp.logical_not(mixed))
    def _():
        terms_ref[:, image_slice(1 - images[0]), :] = jnp.zeros((groups, image_rows, 2 * HD), jnp.bfloat16)


def attention(info, query, out_grad, kv):
    groups, group_rows, _ = kv.shape
    span = groups * group_rows // 2
    vmem = pl.BlockSpec(memory_space=pltpu.VMEM)
    work = 6 * 2 * query.size * span
    return pl.pallas_call(
        attention_kernel,
        out_shape=[
            jax.ShapeDtypeStruct(query.shape, jnp.bfloat16),
            jax.ShapeDtypeStruct(query.shape, jnp.bfloat16),
            jax.ShapeDtypeStruct(kv.shape, jnp.bfloat16),
        ],
        in_specs=[vmem, vmem, vmem, vmem],
        out_specs=[vmem, vmem, vmem],
        scratch_shapes=[
            pltpu.VMEM((2, span, HD), jnp.bfloat16),
            pltpu.VMEM((2, span, HD), jnp.bfloat16),
            pltpu.VMEM((2, span, HD), jnp.float32),
            pltpu.VMEM((2, span, HD), jnp.float32),
        ],
        compiler_params=pltpu.CompilerParams(vmem_limit_bytes=40 * 1024 * 1024),
        cost_estimate=pl.CostEstimate(flops=work, bytes_accessed=5 * 1024 * 1024, transcendentals=query.size * span // HD),
        name="attention",
    )(info, query, out_grad, kv)


def prepare_kernel(seq_index, image_ref, tiles_ref, gain_ref, kv_ref, copies_ref, info_ref, normed_ref, inverse_ref, kept_gain_ref):
    heads = normed_ref.shape[1] // HD
    gain, image, tiles = (gain_ref[...], image_ref[...].astype(jnp.float32), tiles_ref[...].astype(jnp.float32))
    lane = lax.broadcasted_iota(jnp.int32, info_ref.shape, 1)
    begin = seq_index() * 2

    def entry(row, index):
        return jnp.sum(jnp.where(lane == index, row, 0.0), axis=1, keepdims=True)

    info = jnp.where(
        lane == 0,
        entry(image, begin),
        jnp.where(
            lane == 1,
            entry(image, begin + 1),
            jnp.where(lane == 2, entry(tiles, begin), entry(tiles, begin + 1)),
        ),
    )
    info_ref[...] = info
    kept_gain_ref[...] = gain
    for t in range(heads):
        pre = kv_ref[:, 2 * t * HD : (2 * t + 1) * HD].astype(jnp.float32)
        values = kv_ref[:, (2 * t + 1) * HD : (2 * t + 2) * HD]
        inverse = lax.rsqrt(jnp.mean(pre * pre, axis=1, keepdims=True) + epsilon)
        normed = pre * inverse
        keys = (normed * gain).astype(jnp.bfloat16)
        normed_ref[:, t * HD : (t + 1) * HD] = normed
        inverse_ref[:, t * HD : (t + 1) * HD] = jnp.broadcast_to(inverse, normed.shape)
        for copy in range(t, copies_ref.shape[0], heads):
            copies_ref[copy, :, :HD] = keys
            copies_ref[copy, :, HD:] = values


def prepare(seq_index, span_image, span_tiles, key_gain, vision_kv, copies):
    rows, columns = vision_kv.shape
    heads = columns // (2 * HD)
    vmem = pl.BlockSpec(memory_space=pltpu.VMEM)
    return pl.pallas_call(
        functools.partial(prepare_kernel, seq_index),
        out_shape=[
            jax.ShapeDtypeStruct((copies * heads, rows, 2 * HD), jnp.bfloat16),
            jax.ShapeDtypeStruct((1, HD), jnp.float32),
            jax.ShapeDtypeStruct((rows, heads * HD), jnp.float32),
            jax.ShapeDtypeStruct((rows, heads * HD), jnp.float32),
            jax.ShapeDtypeStruct((1, HD), jnp.float32),
        ],
        in_specs=[vmem] * 4,
        out_specs=[vmem] * 5,
        compiler_params=pltpu.CompilerParams(vmem_limit_bytes=8 * 1024 * 1024),
        name="prepare",
    )(span_image.reshape(1, -1), span_tiles.reshape(1, -1), key_gain.reshape(1, -1), vision_kv)


def finish_kernel(got_ref, normed_ref, inverse_ref, gain_ref, out_ref):
    heads = out_ref.shape[1] // (2 * HD)
    gain = gain_ref[...]
    for t in range(heads):
        key_grad, value_grad = (
            sum(got_ref[k, :, part * HD : (part + 1) * HD].astype(jnp.float32) for k in range(t, got_ref.shape[0], heads))
            for part in range(2)
        )
        normed = normed_ref[:, t * HD : (t + 1) * HD]
        inverse = inverse_ref[:, t * HD : (t + 1) * HD]
        scaled = key_grad * gain
        pre_grad = inverse * (scaled - normed * jnp.mean(scaled * normed, axis=1, keepdims=True))
        out_ref[:, 2 * t * HD : (2 * t + 1) * HD] = pre_grad.astype(jnp.bfloat16)
        out_ref[:, (2 * t + 1) * HD : (2 * t + 2) * HD] = value_grad.astype(jnp.bfloat16)


def finish(got, normed, inverse, gain):
    rows = normed.shape[0]
    vmem = pl.BlockSpec(memory_space=pltpu.VMEM)
    return pl.pallas_call(
        finish_kernel,
        out_shape=jax.ShapeDtypeStruct((rows, 2 * normed.shape[1]), jnp.bfloat16),
        in_specs=[vmem] * 4,
        out_specs=vmem,
        compiler_params=pltpu.CompilerParams(vmem_limit_bytes=8 * 1024 * 1024),
        name="finish",
    )(got, normed, inverse, gain)


def spread(rows, axes, copies):
    return lax.all_to_all(
        lax.optimization_barrier(jnp.broadcast_to(rows, (copies,) + rows.shape)), axes, split_axis=0, concat_axis=0
    )


def fold(terms, axis, parts):
    got = lax.all_to_all(terms.reshape((parts, -1) + terms.shape[1:]), axis, split_axis=0, concat_axis=0)
    return jnp.sum(got.astype(jnp.float32), axis=0).astype(jnp.bfloat16)


def body(query, vision_kv, key_gain, out_grad, span_image, span_tiles):
    z, x, cores, tp = (lax.axis_size(name) for name in ("z", "x", "c", "tp"))
    own_rows = vision_kv.shape[0]

    def seq_index():
        return (lax.axis_index("z") * x + lax.axis_index("x")) * cores + lax.axis_index("c")

    copies, info, normed, inverse, gain = prepare(
        seq_index, span_image, span_tiles, key_gain, vision_kv, z
    )
    along_z = lax.all_to_all(copies, ("z", "tp"), split_axis=0, concat_axis=0, tiled=True)
    column = along_z.reshape(z * tp * own_rows, 2 * HD)
    plane = spread(column, "x", x)
    kv = spread(plane, "c", cores).reshape(cores * x, z * tp * own_rows, 2 * HD)

    attn_out, query_grad, terms = attention(info, query, out_grad, kv)

    terms = fold(terms, "c", cores)
    terms = fold(terms, "x", x)
    got = lax.all_to_all(
        terms.reshape(z * tp, own_rows, 2 * HD), ("z", "tp"), split_axis=0, concat_axis=0, tiled=True
    )
    return (attn_out, query_grad, finish(got, normed, inverse, gain))


def solution(mesh):
    fine = Mesh(mesh.devices.reshape(8, 4, 2, 8), ("z", "x", "c", "tp"))
    seq = ("z", "x", "c")
    in_specs = (P(seq, "tp"), P(seq + ("tp",), None), P(), P(seq, "tp"), P(), P())
    out_specs = (P(seq, "tp"), P(seq, "tp"), P(seq + ("tp",), None))
    return jax.shard_map(body, mesh=fine, in_specs=in_specs, out_specs=out_specs, check_vma=False)
```

```python
import functools
import math

import jax
import jax.numpy as jnp
from jax import lax
from jax.experimental import pallas as pl
from jax.experimental.pallas import tpu as pltpu
from jax.sharding import Mesh, PartitionSpec as P

HD = 128
BLOCK = 64
TILES_IMG = 4

epsilon = 1e-05
neg_fill = -1e30
score_scale = 1.0 / math.sqrt(HD)

NN = (((1,), (0,)), ((), ()))
NT = (((1,), (1,)), ((), ()))
TN = (((0,), (0,)), ((), ()))


def dot(a, b, dims):
    return lax.dot_general(a, b, dims, preferred_element_type=jnp.float32)


def attention_kernel(
    image_rows, info_ref, query_ref, grad_ref, kv_ref, out_ref, query_grad_ref, terms_ref,
    key_acc, value_acc, keys_ref, values_ref,
):
    groups, group_rows, _ = kv_ref.shape
    both = group_rows != image_rows
    part = image_rows // TILES_IMG
    span = groups * image_rows
    heads = query_ref.shape[1] // HD
    lane = lax.broadcasted_iota(jnp.int32, info_ref.shape, 1)
    tiles = [jnp.sum(jnp.where(lane == k, info_ref[...], 0.0)).astype(jnp.int32) for k in (2, 3)]
    slots = [0, 0]
    images = [0, 0]
    if both:
        images = [jnp.sum(jnp.where(lane == k, info_ref[...], 0.0)).astype(jnp.int32) for k in range(2)]
        mixed = images[0] != images[1]
        slots = [0, mixed.astype(jnp.int32)]

    def image_slice(image):
        return pl.ds(pl.multiple_of(image * image_rows, image_rows), image_rows) if both else slice(None)

    def view(ref, slot):
        return ref.at[slot] if both else ref

    def load_image(slot, image):
        rows = image_slice(image)
        view(keys_ref, slot)[...] = kv_ref[:, rows, :HD].reshape(span, HD)
        view(values_ref, slot)[...] = kv_ref[:, rows, HD:].reshape(span, HD)

    def keys_of(b):
        return keys_ref[slots[b]] if both else kv_ref[:, :, :HD].reshape(span, HD)

    def values_of(b):
        return values_ref[slots[b]] if both else kv_ref[:, :, HD:].reshape(span, HD)

    def stacked(ref, row, first, count):
        return jnp.concatenate(
            [ref[row : row + BLOCK, j * HD : (j + 1) * HD] for j in range(first, first + count)], axis=0
        )

    def unstack(ref, row, first, count, rows):
        for j in range(count):
            ref[row : row + BLOCK, (first + j) * HD : (first + j + 1) * HD] = rows[j * BLOCK : (j + 1) * BLOCK]

    per_chunk = 4
    column = lax.broadcasted_iota(jnp.int32, (1, span), 1)
    bias = [jnp.where((column & (image_rows - 1)) < n * part, 0.0, neg_fill) for n in tiles]
    live = [(n > 0).astype(jnp.float32) for n in tiles]

    def front(b, first):
        query = stacked(query_ref, b * BLOCK, first, per_chunk)
        grad = stacked(grad_ref, b * BLOCK, first, per_chunk)
        scores = dot(query, keys_of(b), NT) + bias[b]
        prob_grad = dot(grad, values_of(b), NT)
        return query, grad, scores, prob_grad

    def middle(b, first, query, grad, scores, prob_grad):
        row_max = jnp.max(scores, axis=1, keepdims=True)
        terms = jnp.exp((scores - row_max) * score_scale)
        inverse_sum = live[b] / jnp.sum(terms, axis=1, keepdims=True)
        weights = terms * inverse_sum
        probs = weights.astype(jnp.bfloat16)
        out = dot(probs, values_of(b), NN).astype(jnp.bfloat16)
        unstack(out_ref, b * BLOCK, first, per_chunk, out)
        delta = jnp.sum(grad.astype(jnp.float32) * out.astype(jnp.float32), axis=1, keepdims=True)
        dscore = (weights * (prob_grad - delta)).astype(jnp.bfloat16)
        return probs, dscore

    def back(b, first, query, grad, probs, dscore):
        query_grad = (dot(dscore, keys_of(b), NN) * score_scale).astype(jnp.bfloat16)
        unstack(query_grad_ref, b * BLOCK, first, per_chunk, query_grad)
        value_term = dot(probs, grad, TN)
        key_term = dot(dscore, query, TN)
        if b == 0 and first == 0:
            view(value_acc, 0)[...] = value_term
            view(key_acc, 0)[...] = key_term
        else:
            view(value_acc, slots[b])[...] += value_term
            view(key_acc, slots[b])[...] += key_term

    def store_terms(slot, image):
        rows = image_slice(image)
        terms_ref[:, rows, :HD] = (
            (view(key_acc, slot)[...] * score_scale).astype(jnp.bfloat16).reshape(groups, image_rows, HD)
        )
        terms_ref[:, rows, HD:] = view(value_acc, slot)[...].astype(jnp.bfloat16).reshape(groups, image_rows, HD)

    if both:
        load_image(0, images[0])

        @pl.when(mixed)
        def _():
            load_image(1, images[1])
            value_acc[1] = jnp.zeros((span, HD), jnp.float32)
            key_acc[1] = jnp.zeros((span, HD), jnp.float32)

    chunks = [(b, first) for b in range(2) for first in range(0, heads, per_chunk)]
    held = None
    for chunk in chunks:
        query, grad, scores, prob_grad = front(*chunk)
        if held is not None:
            back(*held)
        probs, dscore = middle(*chunk, query, grad, scores, prob_grad)
        held = (*chunk, query, grad, probs, dscore)
    back(*held)
    store_terms(0, images[0])

    if both:

        @pl.when(mixed)
        def _():
            store_terms(1, images[1])

        @pl.when(jnp.logical_not(mixed))
        def _():
            terms_ref[:, image_slice(1 - images[0]), :] = jnp.zeros((groups, image_rows, 2 * HD), jnp.bfloat16)


def attention(info, query, out_grad, kv, image_rows):
    span = kv.shape[0] * image_rows
    slots = kv.shape[1] // image_rows
    held = (slots, span, HD) if slots > 1 else (span, HD)
    scratch = [pltpu.VMEM(held, dtype) for dtype in (jnp.float32, jnp.float32, jnp.bfloat16, jnp.bfloat16)]
    vmem = pl.BlockSpec(memory_space=pltpu.VMEM)
    work = 6 * 2 * query.size * span
    return pl.pallas_call(
        functools.partial(attention_kernel, image_rows),
        out_shape=[
            jax.ShapeDtypeStruct(query.shape, jnp.bfloat16),
            jax.ShapeDtypeStruct(query.shape, jnp.bfloat16),
            jax.ShapeDtypeStruct(kv.shape, jnp.bfloat16),
        ],
        in_specs=[vmem, vmem, vmem, vmem],
        out_specs=[vmem, vmem, vmem],
        scratch_shapes=scratch,
        compiler_params=pltpu.CompilerParams(vmem_limit_bytes=40 * 1024 * 1024),
        cost_estimate=pl.CostEstimate(flops=work, bytes_accessed=5 * 1024 * 1024, transcendentals=query.size * span // HD),
        name="attention",
    )(info, query, out_grad, kv)


def prepare_kernel(
    mesh_index, image_ref, tiles_ref, gain_ref, kv_ref,
    copies_ref, info_ref, plane_ref, normed_ref, inverse_ref, kept_gain_ref,
):
    heads = normed_ref.shape[1] // HD
    gain, image, tiles = (gain_ref[...], image_ref[...].astype(jnp.float32), tiles_ref[...].astype(jnp.float32))
    lane = lax.broadcasted_iota(jnp.int32, info_ref.shape, 1)
    plane, place, cores = mesh_index()
    begin = (plane + place) * 2

    def entry(row, index):
        return jnp.sum(jnp.where(lane == index, row, 0.0), axis=1, keepdims=True)

    info = jnp.where(
        lane == 0,
        entry(image, begin),
        jnp.where(
            lane == 1,
            entry(image, begin + 1),
            jnp.where(lane == 2, entry(tiles, begin), entry(tiles, begin + 1)),
        ),
    )
    mixed = jnp.sum(jnp.where((lane & 1) == 1, image, -image), axis=1, keepdims=True)
    info_ref[...] = info
    members = plane_ref.shape[0]
    member = lax.broadcasted_iota(jnp.int32, (members, HD), 0)
    member_lane = lax.broadcasted_iota(jnp.int32, (members, HD), 1)
    first = plane * 2
    for core in range(cores):
        place = member - core * (members // cores)
        first = first + jnp.where((place >= 0) & (place < members // cores), (place * cores + core) * 2, 0)
    seen = jnp.sum(jnp.where(member_lane == first, image, 0.0), axis=1, keepdims=True)
    plane_ref[...] = jnp.broadcast_to(seen, plane_ref.shape)
    kept_gain_ref[...] = gain
    for t in range(heads):
        pre = kv_ref[:, 2 * t * HD : (2 * t + 1) * HD].astype(jnp.float32)
        values = kv_ref[:, (2 * t + 1) * HD : (2 * t + 2) * HD]
        inverse = lax.rsqrt(jnp.mean(pre * pre, axis=1, keepdims=True) + epsilon)
        normed = pre * inverse
        keys = (normed * gain).astype(jnp.bfloat16)
        normed_ref[:, t * HD : (t + 1) * HD] = normed
        inverse_ref[:, t * HD : (t + 1) * HD] = jnp.broadcast_to(inverse, normed.shape)
        for copy in range(t, copies_ref.shape[0], heads):
            copies_ref[copy, :, :HD] = keys
            copies_ref[copy, :, HD:] = values


def prepare(mesh_index, members, span_image, span_tiles, key_gain, vision_kv, copies):
    rows, columns = vision_kv.shape
    heads = columns // (2 * HD)
    vmem = pl.BlockSpec(memory_space=pltpu.VMEM)
    return pl.pallas_call(
        functools.partial(prepare_kernel, mesh_index),
        out_shape=[
            jax.ShapeDtypeStruct((copies * heads, rows, 2 * HD), jnp.bfloat16),
            jax.ShapeDtypeStruct((1, HD), jnp.float32),
            jax.ShapeDtypeStruct((members, 2 * HD), jnp.float32),
            jax.ShapeDtypeStruct((rows, heads * HD), jnp.float32),
            jax.ShapeDtypeStruct((rows, heads * HD), jnp.float32),
            jax.ShapeDtypeStruct((1, HD), jnp.float32),
        ],
        in_specs=[vmem] * 4,
        out_specs=[vmem] * 6,
        compiler_params=pltpu.CompilerParams(vmem_limit_bytes=8 * 1024 * 1024),
        name="prepare",
    )(span_image.reshape(1, -1), span_tiles.reshape(1, -1), key_gain.reshape(1, -1), vision_kv)


def finish_kernel(got_ref, normed_ref, inverse_ref, gain_ref, out_ref):
    heads = out_ref.shape[1] // (2 * HD)
    gain = gain_ref[...]
    for t in range(heads):
        key_grad, value_grad = (
            sum(got_ref[k, :, part * HD : (part + 1) * HD].astype(jnp.float32) for k in range(t, got_ref.shape[0], heads))
            for part in range(2)
        )
        normed = normed_ref[:, t * HD : (t + 1) * HD]
        inverse = inverse_ref[:, t * HD : (t + 1) * HD]
        scaled = key_grad * gain
        pre_grad = inverse * (scaled - normed * jnp.mean(scaled * normed, axis=1, keepdims=True))
        out_ref[:, 2 * t * HD : (2 * t + 1) * HD] = pre_grad.astype(jnp.bfloat16)
        out_ref[:, (2 * t + 1) * HD : (2 * t + 2) * HD] = value_grad.astype(jnp.bfloat16)


def finish(got, normed, inverse, gain):
    rows = normed.shape[0]
    vmem = pl.BlockSpec(memory_space=pltpu.VMEM)
    return pl.pallas_call(
        finish_kernel,
        out_shape=jax.ShapeDtypeStruct((rows, 2 * normed.shape[1]), jnp.bfloat16),
        in_specs=[vmem] * 4,
        out_specs=vmem,
        compiler_params=pltpu.CompilerParams(vmem_limit_bytes=8 * 1024 * 1024),
        name="finish",
    )(got, normed, inverse, gain)


def route_kernel(plane_ref, column_ref, out_ref):
    members, image_rows, _ = out_ref.shape
    first = column_ref[:image_rows, :]
    second = column_ref[image_rows:, :]
    for k in range(members):
        out_ref[k] = jnp.where(plane_ref[k : k + 1, :] > 0.5, second, first)


def collect_kernel(plane_ref, got_ref, out_ref):
    members, image_rows, _ = got_ref.shape
    totals = [0.0, 0.0]
    for k in range(members):
        term = got_ref[k].astype(jnp.float32)
        second = plane_ref[k : k + 1, :] > 0.5
        totals = [totals[0] + jnp.where(second, 0.0, term), totals[1] + jnp.where(second, term, 0.0)]
    for image in range(2):
        out_ref[image * image_rows : (image + 1) * image_rows, :] = totals[image].astype(jnp.bfloat16)


def small_call(kernel, shape, *args):
    vmem = pl.BlockSpec(memory_space=pltpu.VMEM)
    return pl.pallas_call(
        kernel,
        out_shape=jax.ShapeDtypeStruct(shape, jnp.bfloat16),
        in_specs=[vmem] * len(args),
        out_specs=vmem,
        compiler_params=pltpu.CompilerParams(vmem_limit_bytes=8 * 1024 * 1024),
        name=kernel.__name__,
    )(*args)


def spread(rows, axes, copies):
    return lax.all_to_all(
        lax.optimization_barrier(jnp.broadcast_to(rows, (copies,) + rows.shape)), axes, split_axis=0, concat_axis=0
    )


def fold(terms, axis, parts):
    got = lax.all_to_all(terms.reshape((parts, -1) + terms.shape[1:]), axis, split_axis=0, concat_axis=0)
    return jnp.sum(got.astype(jnp.float32), axis=0).astype(jnp.bfloat16)


def body(query, vision_kv, key_gain, out_grad, span_image, span_tiles):
    z, x, cores, tp = (lax.axis_size(name) for name in ("z", "x", "c", "tp"))
    own_rows = vision_kv.shape[0]
    column_rows = z * tp * own_rows
    image_rows = column_rows // 2
    members = x * cores

    def mesh_index():
        return lax.axis_index("z") * members, lax.axis_index("x") * cores + lax.axis_index("c"), cores

    mixed = jnp.sum(jnp.where(jnp.arange(span_image.shape[0]) % 2 == 1, span_image, -span_image)) > 0

    copies, info, plane, normed, inverse, gain = prepare(
        mesh_index, members, span_image, span_tiles, key_gain, vision_kv, z
    )
    along_z = lax.all_to_all(copies, ("z", "tp"), split_axis=0, concat_axis=0, tiled=True)
    column = along_z.reshape(column_rows, 2 * HD)

    def one_image(info, plane, column, query, out_grad):
        routed = small_call(route_kernel, (members, image_rows, 2 * HD), plane, column)
        kv = lax.all_to_all(routed, ("c", "x"), split_axis=0, concat_axis=0, tiled=True)
        attn_out, query_grad, terms = attention(info, query, out_grad, kv, image_rows)
        got = lax.all_to_all(terms, ("c", "x"), split_axis=0, concat_axis=0, tiled=True)
        return attn_out, query_grad, small_call(collect_kernel, column.shape, plane, got)

    def two_images(info, plane, column, query, out_grad):
        kv = spread(spread(column, "x", x), "c", cores).reshape(members, column_rows, 2 * HD)
        attn_out, query_grad, terms = attention(info, query, out_grad, kv, image_rows)
        return attn_out, query_grad, fold(fold(terms, "c", cores), "x", x).reshape(column.shape)

    attn_out, query_grad, terms = lax.cond(
        mixed, two_images, one_image, info, plane, column, query, out_grad
    )
    got = lax.all_to_all(
        terms.reshape(z * tp, own_rows, 2 * HD), ("z", "tp"), split_axis=0, concat_axis=0, tiled=True
    )
    return (attn_out, query_grad, finish(got, normed, inverse, gain))


def solution(mesh):
    fine = Mesh(mesh.devices.reshape(8, 4, 2, 8), ("z", "x", "c", "tp"))
    seq = ("z", "x", "c")
    in_specs = (P(seq, "tp"), P(seq + ("tp",), None), P(), P(seq, "tp"), P(), P())
    out_specs = (P(seq, "tp"), P(seq, "tp"), P(seq + ("tp",), None))
    return jax.shard_map(body, mesh=fine, in_specs=in_specs, out_specs=out_specs, check_vma=False)
```

```python
import functools
import math

import jax
import jax.numpy as jnp
from jax import lax
from jax.experimental import pallas as pl
from jax.experimental.pallas import tpu as pltpu
from jax.sharding import Mesh, PartitionSpec as P

HD = 128
BLOCK = 64
TILES_IMG = 4

epsilon = 1e-05
neg_fill = -1e30
score_scale = 1.0 / math.sqrt(HD)

NN = (((1,), (0,)), ((), ()))
NT = (((1,), (1,)), ((), ()))
TN = (((0,), (0,)), ((), ()))


def dot(a, b, dims):
    return lax.dot_general(a, b, dims, preferred_element_type=jnp.float32)


def attention_kernel(further, info_ref, query_ref, grad_ref, *refs):
    come_ref = back_ref = None
    if further:
        come_ref, kv_ref, out_ref, query_grad_ref, back_ref, terms_ref, key_acc, value_acc = refs
    else:
        kv_ref, out_ref, query_grad_ref, terms_ref, key_acc, value_acc = refs
    groups, group_rows, _ = kv_ref.shape
    part = group_rows // TILES_IMG
    span = groups * group_rows
    heads = query_ref.shape[1] // HD
    lane = lax.broadcasted_iota(jnp.int32, info_ref.shape, 1)
    tiles = [jnp.sum(jnp.where(lane == k, info_ref[...], 0.0)).astype(jnp.int32) for k in range(2)]

    def keys():
        return kv_ref[:, :, :HD].reshape(span, HD)

    def values():
        return kv_ref[:, :, HD:].reshape(span, HD)

    def block_of(ref, other_ref, which, b):
        if further and b == 1:
            return other_ref.at[which]
        return ref.at[pl.ds((1 if further else b) * BLOCK, BLOCK)]

    def stacked(rows, first, count):
        return jnp.concatenate([rows[:, j * HD : (j + 1) * HD] for j in range(first, first + count)], axis=0)

    def unstack(rows, first, count, value):
        for j in range(count):
            rows[:, (first + j) * HD : (first + j + 1) * HD] = value[j * BLOCK : (j + 1) * BLOCK]

    per_chunk = 4
    column = lax.broadcasted_iota(jnp.int32, (1, span), 1)
    bias = [jnp.where((column & (group_rows - 1)) < n * part, 0.0, neg_fill) for n in tiles]
    live = [(n > 0).astype(jnp.float32) for n in tiles]

    def front(b, first):
        query = stacked(block_of(query_ref, come_ref, 0, b), first, per_chunk)
        grad = stacked(block_of(grad_ref, come_ref, 1, b), first, per_chunk)
        scores = dot(query, keys(), NT) + bias[b]
        prob_grad = dot(grad, values(), NT)
        return query, grad, scores, prob_grad

    def middle(b, first, query, grad, scores, prob_grad):
        row_max = jnp.max(scores, axis=1, keepdims=True)
        terms = jnp.exp((scores - row_max) * score_scale)
        inverse_sum = live[b] / jnp.sum(terms, axis=1, keepdims=True)
        weights = terms * inverse_sum
        probs = weights.astype(jnp.bfloat16)
        out = dot(probs, values(), NN).astype(jnp.bfloat16)
        unstack(block_of(out_ref, back_ref, 0, b), first, per_chunk, out)
        delta = jnp.sum(grad.astype(jnp.float32) * out.astype(jnp.float32), axis=1, keepdims=True)
        dscore = (weights * (prob_grad - delta)).astype(jnp.bfloat16)
        return probs, dscore

    def back(b, first, query, grad, probs, dscore):
        query_grad = (dot(dscore, keys(), NN) * score_scale).astype(jnp.bfloat16)
        unstack(block_of(query_grad_ref, back_ref, 1, b), first, per_chunk, query_grad)
        value_term = dot(probs, grad, TN)
        key_term = dot(dscore, query, TN)
        if b == 0 and first == 0:
            value_acc[...] = value_term
            key_acc[...] = key_term
        else:
            value_acc[...] += value_term
            key_acc[...] += key_term

    chunks = [(b, first) for b in range(2) for first in range(0, heads, per_chunk)]
    held = None
    for chunk in chunks:
        query, grad, scores, prob_grad = front(*chunk)
        if held is not None:
            back(*held)
        probs, dscore = middle(*chunk, query, grad, scores, prob_grad)
        held = (*chunk, query, grad, probs, dscore)
    back(*held)
    terms_ref[:, :, :HD] = (key_acc[...] * score_scale).astype(jnp.bfloat16).reshape(groups, group_rows, HD)
    terms_ref[:, :, HD:] = value_acc[...].astype(jnp.bfloat16).reshape(groups, group_rows, HD)


def attention(info, query, out_grad, kv, come=None):
    span = kv.shape[0] * kv.shape[1]
    vmem = pl.BlockSpec(memory_space=pltpu.VMEM)
    work = 6 * 2 * query.size * span
    moved = [] if come is None else [come]
    args = [info, query, out_grad, *moved, kv]
    shapes = [query.shape, query.shape, *(array.shape for array in moved), kv.shape]
    return pl.pallas_call(
        functools.partial(attention_kernel, come is not None),
        out_shape=[jax.ShapeDtypeStruct(shape, jnp.bfloat16) for shape in shapes],
        in_specs=[vmem] * len(args),
        out_specs=[vmem] * len(shapes),
        scratch_shapes=[pltpu.VMEM((span, HD), jnp.float32)] * 2,
        compiler_params=pltpu.CompilerParams(vmem_limit_bytes=40 * 1024 * 1024),
        cost_estimate=pl.CostEstimate(flops=work, bytes_accessed=5 * 1024 * 1024, transcendentals=query.size * span // HD),
        name="attention",
    )(*args)


def prepare_kernel(
    mesh_index, image_ref, tiles_ref, gain_ref, kv_ref,
    copies_ref, info_ref, plane_ref, normed_ref, inverse_ref, kept_gain_ref,
):
    heads = normed_ref.shape[1] // HD
    gain, image, tiles = (gain_ref[...], image_ref[...].astype(jnp.float32), tiles_ref[...].astype(jnp.float32))
    lane = lax.broadcasted_iota(jnp.int32, info_ref.shape, 1)
    plane, place, cores = mesh_index()
    begin = (plane + place) * 2

    blocks = image.shape[1]
    mixed = jnp.sum(jnp.where((lane & 1) == 1, image, -image), axis=1, keepdims=True)
    begin = begin + (mixed > 0.5).astype(jnp.int32)

    def entry(row, index):
        return jnp.sum(jnp.where(lane == (index & (blocks - 1)), row, 0.0), axis=1, keepdims=True)

    info_ref[...] = jnp.where(
        lane == 0, entry(tiles, begin), jnp.where(lane == 1, entry(tiles, begin + 1), jnp.where(lane == 2, mixed, 0.0))
    )
    members = plane_ref.shape[0]
    member = lax.broadcasted_iota(jnp.int32, (members, blocks), 0)
    member_lane = lax.broadcasted_iota(jnp.int32, (members, blocks), 1)
    first = plane * 2 + (mixed > 0.5).astype(jnp.int32)
    for core in range(cores):
        upper = member - core * (members // cores)
        first = first + jnp.where((upper >= 0) & (upper < members // cores), (upper * cores + core) * 2, 0)
    seen = jnp.sum(jnp.where(member_lane == first, image, 0.0), axis=1, keepdims=True)
    plane_ref[...] = jnp.broadcast_to(seen, plane_ref.shape)
    kept_gain_ref[...] = gain
    for t in range(heads):
        pre = kv_ref[:, 2 * t * HD : (2 * t + 1) * HD].astype(jnp.float32)
        values = kv_ref[:, (2 * t + 1) * HD : (2 * t + 2) * HD]
        inverse = lax.rsqrt(jnp.mean(pre * pre, axis=1, keepdims=True) + epsilon)
        normed = pre * inverse
        keys = (normed * gain).astype(jnp.bfloat16)
        normed_ref[:, t * HD : (t + 1) * HD] = normed
        inverse_ref[:, t * HD : (t + 1) * HD] = jnp.broadcast_to(inverse, normed.shape)
        for copy in range(t, copies_ref.shape[0], heads):
            copies_ref[copy, :, :HD] = keys
            copies_ref[copy, :, HD:] = values


def prepare(mesh_index, members, span_image, span_tiles, key_gain, vision_kv, copies):
    rows, columns = vision_kv.shape
    heads = columns // (2 * HD)
    vmem = pl.BlockSpec(memory_space=pltpu.VMEM)
    return pl.pallas_call(
        functools.partial(prepare_kernel, mesh_index),
        out_shape=[
            jax.ShapeDtypeStruct((copies * heads, rows, 2 * HD), jnp.bfloat16),
            jax.ShapeDtypeStruct((1, HD), jnp.float32),
            jax.ShapeDtypeStruct((members, 2 * HD), jnp.float32),
            jax.ShapeDtypeStruct((rows, heads * HD), jnp.float32),
            jax.ShapeDtypeStruct((rows, heads * HD), jnp.float32),
            jax.ShapeDtypeStruct((1, HD), jnp.float32),
        ],
        in_specs=[vmem] * 4,
        out_specs=[vmem] * 6,
        compiler_params=pltpu.CompilerParams(vmem_limit_bytes=8 * 1024 * 1024),
        name="prepare",
    )(span_image.reshape(1, -1), span_tiles.reshape(1, -1), key_gain.reshape(1, -1), vision_kv)


def finish_kernel(got_ref, normed_ref, inverse_ref, gain_ref, out_ref):
    heads = out_ref.shape[1] // (2 * HD)
    gain = gain_ref[...]
    for t in range(heads):
        key_grad, value_grad = (
            sum(got_ref[k, :, part * HD : (part + 1) * HD].astype(jnp.float32) for k in range(t, got_ref.shape[0], heads))
            for part in range(2)
        )
        normed = normed_ref[:, t * HD : (t + 1) * HD]
        inverse = inverse_ref[:, t * HD : (t + 1) * HD]
        scaled = key_grad * gain
        pre_grad = inverse * (scaled - normed * jnp.mean(scaled * normed, axis=1, keepdims=True))
        out_ref[:, 2 * t * HD : (2 * t + 1) * HD] = pre_grad.astype(jnp.bfloat16)
        out_ref[:, (2 * t + 1) * HD : (2 * t + 2) * HD] = value_grad.astype(jnp.bfloat16)


def finish(got, normed, inverse, gain):
    rows = normed.shape[0]
    vmem = pl.BlockSpec(memory_space=pltpu.VMEM)
    return pl.pallas_call(
        finish_kernel,
        out_shape=jax.ShapeDtypeStruct((rows, 2 * normed.shape[1]), jnp.bfloat16),
        in_specs=[vmem] * 4,
        out_specs=vmem,
        compiler_params=pltpu.CompilerParams(vmem_limit_bytes=8 * 1024 * 1024),
        name="finish",
    )(got, normed, inverse, gain)


def route_kernel(plane_ref, column_ref, out_ref):
    members, image_rows, _ = out_ref.shape
    first = column_ref[:image_rows, :]
    second = column_ref[image_rows:, :]
    for k in range(members):
        out_ref[k] = jnp.where(plane_ref[k : k + 1, :] > 0.5, second, first)


def collect_kernel(plane_ref, got_ref, out_ref):
    members, image_rows, _ = got_ref.shape
    totals = [0.0, 0.0]
    for k in range(members):
        term = got_ref[k].astype(jnp.float32)
        second = plane_ref[k : k + 1, :] > 0.5
        totals = [totals[0] + jnp.where(second, 0.0, term), totals[1] + jnp.where(second, term, 0.0)]
    for image in range(2):
        out_ref[image * image_rows : (image + 1) * image_rows, :] = totals[image].astype(jnp.bfloat16)


def small_call(kernel, shape, *args):
    vmem = pl.BlockSpec(memory_space=pltpu.VMEM)
    return pl.pallas_call(
        kernel,
        out_shape=jax.ShapeDtypeStruct(shape, jnp.bfloat16),
        in_specs=[vmem] * len(args),
        out_specs=vmem,
        compiler_params=pltpu.CompilerParams(vmem_limit_bytes=8 * 1024 * 1024),
        name=kernel.__name__,
    )(*args)


def body(query, vision_kv, key_gain, out_grad, span_image, span_tiles):
    z, x, cores, tp = (lax.axis_size(name) for name in ("z", "x", "c", "tp"))
    own_rows = vision_kv.shape[0]
    column_rows = z * tp * own_rows
    image_rows = column_rows // 2
    members = x * cores

    def mesh_index():
        return lax.axis_index("z") * members, lax.axis_index("x") * cores + lax.axis_index("c"), cores

    mixed = jnp.sum(jnp.where(jnp.arange(span_image.shape[0]) % 2 == 1, span_image, -span_image)) > 0

    copies, info, plane, normed, inverse, gain = prepare(
        mesh_index, members, span_image, span_tiles, key_gain, vision_kv, z
    )
    along_z = lax.all_to_all(copies, ("z", "tp"), split_axis=0, concat_axis=0, tiled=True)
    column = along_z.reshape(column_rows, 2 * HD)

    def pass_on(blocks, step):
        count = z * members
        return lax.ppermute(blocks, ("z", "x", "c"), [(source, (source + step) % count) for source in range(count)])

    def travel(plane, column):
        routed = small_call(route_kernel, (members, image_rows, 2 * HD), plane, column)
        return lax.all_to_all(routed, ("c", "x"), split_axis=0, concat_axis=0, tiled=True)

    def travel_back(plane, terms):
        got = lax.all_to_all(terms, ("c", "x"), split_axis=0, concat_axis=0, tiled=True)
        return small_call(collect_kernel, column.shape, plane, got)

    def own_blocks(info, plane, column, query, out_grad):
        attn_out, query_grad, terms = attention(info, query, out_grad, travel(plane, column))
        return attn_out, query_grad, travel_back(plane, terms)

    def blocks_further(info, plane, column, query, out_grad):
        come = pass_on(jnp.stack([query[:BLOCK], out_grad[:BLOCK]]), -1)
        attn_out, query_grad, back, terms = attention(info, query, out_grad, travel(plane, column), come)
        home = pass_on(back, 1)
        terms = travel_back(plane, terms)
        return attn_out.at[:BLOCK].set(home[0]), query_grad.at[:BLOCK].set(home[1]), terms

    attn_out, query_grad, terms = lax.cond(
        mixed, blocks_further, own_blocks, info, plane, column, query, out_grad
    )
    got = lax.all_to_all(
        terms.reshape(z * tp, own_rows, 2 * HD), ("z", "tp"), split_axis=0, concat_axis=0, tiled=True
    )
    return (attn_out, query_grad, finish(got, normed, inverse, gain))


def solution(mesh):
    fine = Mesh(mesh.devices.reshape(8, 4, 2, 8), ("z", "x", "c", "tp"))
    seq = ("z", "x", "c")
    in_specs = (P(seq, "tp"), P(seq + ("tp",), None), P(), P(seq, "tp"), P(), P())
    out_specs = (P(seq, "tp"), P(seq, "tp"), P(seq + ("tp",), None))
    return jax.shard_map(body, mesh=fine, in_specs=in_specs, out_specs=out_specs, check_vma=False)
```

```python
import functools
import math

import jax
import jax.numpy as jnp
from jax import lax
from jax.experimental import pallas as pl
from jax.experimental.pallas import tpu as pltpu
from jax.sharding import Mesh, PartitionSpec as P

HD = 128
BLOCK = 64
TILES_IMG = 4

epsilon = 1e-05
neg_fill = -1e30
score_scale = 1.0 / math.sqrt(HD)

NN = (((1,), (0,)), ((), ()))
NT = (((1,), (1,)), ((), ()))
TN = (((0,), (0,)), ((), ()))


def dot(a, b, dims):
    return lax.dot_general(a, b, dims, preferred_element_type=jnp.float32)


def attention_kernel(further, info_ref, query_ref, grad_ref, *refs):
    come_ref = back_ref = None
    if further:
        come_ref, kv_ref, out_ref, query_grad_ref, back_ref, terms_ref, key_acc, value_acc = refs
    else:
        kv_ref, out_ref, query_grad_ref, terms_ref, key_acc, value_acc = refs
    groups, group_rows, _ = kv_ref.shape
    part = group_rows // TILES_IMG
    span = groups * group_rows
    heads = query_ref.shape[1] // HD
    lane = lax.broadcasted_iota(jnp.int32, info_ref.shape, 1)
    tiles = [jnp.sum(jnp.where(lane == k, info_ref[...], 0.0)).astype(jnp.int32) for k in range(2)]

    def keys():
        return kv_ref[:, :, :HD].reshape(span, HD)

    def values():
        return kv_ref[:, :, HD:].reshape(span, HD)

    def block_of(ref, other_ref, which, b):
        if further and b == 1:
            return other_ref.at[which]
        return ref.at[pl.ds((1 if further else b) * BLOCK, BLOCK)]

    def stacked(rows, first, count):
        return jnp.concatenate([rows[:, j * HD : (j + 1) * HD] for j in range(first, first + count)], axis=0)

    def unstack(rows, first, count, value):
        for j in range(count):
            rows[:, (first + j) * HD : (first + j + 1) * HD] = value[j * BLOCK : (j + 1) * BLOCK]

    per_chunk = 4
    column = lax.broadcasted_iota(jnp.int32, (1, span), 1)
    bias = [jnp.where((column & (group_rows - 1)) < n * part, 0.0, neg_fill) for n in tiles]
    live = [(n > 0).astype(jnp.float32) for n in tiles]

    def front(b, first):
        query = stacked(block_of(query_ref, come_ref, 0, b), first, per_chunk)
        grad = stacked(block_of(grad_ref, come_ref, 1, b), first, per_chunk)
        scores = dot(query, keys(), NT) + bias[b]
        prob_grad = dot(grad, values(), NT)
        return query, grad, scores, prob_grad

    def middle(b, first, query, grad, scores, prob_grad):
        row_max = jnp.max(scores, axis=1, keepdims=True)
        terms = jnp.exp((scores - row_max) * score_scale)
        inverse_sum = live[b] / jnp.sum(terms, axis=1, keepdims=True)
        weights = terms * inverse_sum
        probs = weights.astype(jnp.bfloat16)
        out = dot(probs, values(), NN).astype(jnp.bfloat16)
        unstack(block_of(out_ref, back_ref, 0, b), first, per_chunk, out)
        delta = jnp.sum(grad.astype(jnp.float32) * out.astype(jnp.float32), axis=1, keepdims=True)
        dscore = (weights * (prob_grad - delta)).astype(jnp.bfloat16)
        return probs, dscore

    def back(b, first, query, grad, probs, dscore):
        query_grad = (dot(dscore, keys(), NN) * score_scale).astype(jnp.bfloat16)
        unstack(block_of(query_grad_ref, back_ref, 1, b), first, per_chunk, query_grad)
        value_term = dot(probs, grad, TN)
        key_term = dot(dscore, query, TN)
        if b == 0 and first == 0:
            value_acc[...] = value_term
            key_acc[...] = key_term
        else:
            value_acc[...] += value_term
            key_acc[...] += key_term

    chunks = [(b, first) for b in range(2) for first in range(0, heads, per_chunk)]
    held = None
    for chunk in chunks:
        query, grad, scores, prob_grad = front(*chunk)
        if held is not None:
            back(*held)
        probs, dscore = middle(*chunk, query, grad, scores, prob_grad)
        held = (*chunk, query, grad, probs, dscore)
    back(*held)
    terms_ref[:, :, :HD] = (key_acc[...] * score_scale).astype(jnp.bfloat16).reshape(groups, group_rows, HD)
    terms_ref[:, :, HD:] = value_acc[...].astype(jnp.bfloat16).reshape(groups, group_rows, HD)


def attention(info, query, out_grad, kv, come=None):
    span = kv.shape[0] * kv.shape[1]
    vmem = pl.BlockSpec(memory_space=pltpu.VMEM)
    work = 6 * 2 * query.size * span
    moved = [] if come is None else [come]
    args = [info, query, out_grad, *moved, kv]
    shapes = [query.shape, query.shape, *(array.shape for array in moved), kv.shape]
    return pl.pallas_call(
        functools.partial(attention_kernel, come is not None),
        out_shape=[jax.ShapeDtypeStruct(shape, jnp.bfloat16) for shape in shapes],
        in_specs=[vmem] * len(args),
        out_specs=[vmem] * len(shapes),
        scratch_shapes=[pltpu.VMEM((span, HD), jnp.float32)] * 2,
        compiler_params=pltpu.CompilerParams(vmem_limit_bytes=40 * 1024 * 1024),
        cost_estimate=pl.CostEstimate(flops=work, bytes_accessed=5 * 1024 * 1024, transcendentals=query.size * span // HD),
        name="attention",
    )(*args)


def prepare_kernel(kv_ref, copies_ref, normed_ref, inverse_ref):
    heads = normed_ref.shape[1] // HD
    for t in range(heads):
        pre = kv_ref[:, 2 * t * HD : (2 * t + 1) * HD].astype(jnp.float32)
        inverse = lax.rsqrt(jnp.mean(pre * pre, axis=1, keepdims=True) + epsilon)
        normed_ref[:, t * HD : (t + 1) * HD] = pre * inverse
        inverse_ref[:, t * HD : (t + 1) * HD] = jnp.broadcast_to(inverse, pre.shape)
        for copy in range(t, copies_ref.shape[0], heads):
            copies_ref[copy] = kv_ref[:, 2 * t * HD : (2 * t + 2) * HD]


def prepare(vision_kv, copies):
    rows, columns = vision_kv.shape
    heads = columns // (2 * HD)
    vmem = pl.BlockSpec(memory_space=pltpu.VMEM)
    return pl.pallas_call(
        prepare_kernel,
        out_shape=[
            jax.ShapeDtypeStruct((copies * heads, rows, 2 * HD), jnp.bfloat16),
            jax.ShapeDtypeStruct((rows, heads * HD), jnp.float32),
            jax.ShapeDtypeStruct((rows, heads * HD), jnp.float32),
        ],
        in_specs=[vmem],
        out_specs=[vmem] * 3,
        compiler_params=pltpu.CompilerParams(vmem_limit_bytes=8 * 1024 * 1024),
        name="prepare",
    )(vision_kv)


def look_kernel(mesh_index, image_ref, tiles_ref, gain_ref, info_ref, plane_ref, kept_gain_ref):
    image, tiles = image_ref[...].astype(jnp.float32), tiles_ref[...].astype(jnp.float32)
    kept_gain_ref[...] = gain_ref[...]
    lane = lax.broadcasted_iota(jnp.int32, info_ref.shape, 1)
    plane, place, cores = mesh_index()
    begin = (plane + place) * 2
    blocks = image.shape[1]
    mixed = jnp.sum(jnp.where((lane & 1) == 1, image, -image), axis=1, keepdims=True)
    begin = begin + (mixed > 0.5).astype(jnp.int32)

    def entry(row, index):
        return jnp.sum(jnp.where(lane == (index & (blocks - 1)), row, 0.0), axis=1, keepdims=True)

    info_ref[...] = jnp.where(
        lane == 0, entry(tiles, begin), jnp.where(lane == 1, entry(tiles, begin + 1), jnp.where(lane == 2, mixed, 0.0))
    )
    members = plane_ref.shape[0]
    member = lax.broadcasted_iota(jnp.int32, (members, blocks), 0)
    member_lane = lax.broadcasted_iota(jnp.int32, (members, blocks), 1)
    first = plane * 2 + (mixed > 0.5).astype(jnp.int32)
    for core in range(cores):
        upper = member - core * (members // cores)
        first = first + jnp.where((upper >= 0) & (upper < members // cores), (upper * cores + core) * 2, 0)
    seen = jnp.sum(jnp.where(member_lane == first, image, 0.0), axis=1, keepdims=True)
    plane_ref[...] = jnp.broadcast_to(seen, plane_ref.shape)


def look(mesh_index, members, span_image, span_tiles, key_gain):
    vmem = pl.BlockSpec(memory_space=pltpu.VMEM)
    return pl.pallas_call(
        functools.partial(look_kernel, mesh_index),
        out_shape=[
            jax.ShapeDtypeStruct((1, HD), jnp.float32),
            jax.ShapeDtypeStruct((members, 2 * HD), jnp.float32),
            jax.ShapeDtypeStruct((1, HD), jnp.float32),
        ],
        in_specs=[vmem] * 3,
        out_specs=[vmem] * 3,
        compiler_params=pltpu.CompilerParams(vmem_limit_bytes=8 * 1024 * 1024),
        name="look",
    )(span_image.reshape(1, -1), span_tiles.reshape(1, -1), key_gain.reshape(1, -1))


def finish_kernel(got_ref, normed_ref, inverse_ref, gain_ref, out_ref):
    heads = out_ref.shape[1] // (2 * HD)
    gain = gain_ref[...]
    for t in range(heads):
        key_grad, value_grad = (
            sum(got_ref[k, :, part * HD : (part + 1) * HD].astype(jnp.float32) for k in range(t, got_ref.shape[0], heads))
            for part in range(2)
        )
        normed = normed_ref[:, t * HD : (t + 1) * HD]
        inverse = inverse_ref[:, t * HD : (t + 1) * HD]
        scaled = key_grad * gain
        pre_grad = inverse * (scaled - normed * jnp.mean(scaled * normed, axis=1, keepdims=True))
        out_ref[:, 2 * t * HD : (2 * t + 1) * HD] = pre_grad.astype(jnp.bfloat16)
        out_ref[:, (2 * t + 1) * HD : (2 * t + 2) * HD] = value_grad.astype(jnp.bfloat16)


def finish(got, normed, inverse, gain):
    rows = normed.shape[0]
    vmem = pl.BlockSpec(memory_space=pltpu.VMEM)
    return pl.pallas_call(
        finish_kernel,
        out_shape=jax.ShapeDtypeStruct((rows, 2 * normed.shape[1]), jnp.bfloat16),
        in_specs=[vmem] * 4,
        out_specs=vmem,
        compiler_params=pltpu.CompilerParams(vmem_limit_bytes=8 * 1024 * 1024),
        name="finish",
    )(got, normed, inverse, gain)


def route_kernel(plane_ref, gain_ref, column_ref, out_ref):
    members, image_rows, _ = out_ref.shape
    pre = column_ref[:, :HD].astype(jnp.float32)
    inverse = lax.rsqrt(jnp.mean(pre * pre, axis=1, keepdims=True) + epsilon)
    keys = (pre * inverse * gain_ref[...]).astype(jnp.bfloat16)
    for half, rows in enumerate((keys, column_ref[:, HD:])):
        part = slice(half * HD, (half + 1) * HD)
        for k in range(members):
            out_ref[k, :, part] = jnp.where(plane_ref[k : k + 1, part] > 0.5, rows[image_rows:], rows[:image_rows])


def collect_kernel(plane_ref, got_ref, out_ref):
    members, image_rows, _ = got_ref.shape
    totals = [0.0, 0.0]
    for k in range(members):
        term = got_ref[k].astype(jnp.float32)
        second = plane_ref[k : k + 1, :] > 0.5
        totals = [totals[0] + jnp.where(second, 0.0, term), totals[1] + jnp.where(second, term, 0.0)]
    for image in range(2):
        out_ref[image * image_rows : (image + 1) * image_rows, :] = totals[image].astype(jnp.bfloat16)


def small_call(kernel, shape, *args):
    vmem = pl.BlockSpec(memory_space=pltpu.VMEM)
    return pl.pallas_call(
        kernel,
        out_shape=jax.ShapeDtypeStruct(shape, jnp.bfloat16),
        in_specs=[vmem] * len(args),
        out_specs=vmem,
        compiler_params=pltpu.CompilerParams(vmem_limit_bytes=8 * 1024 * 1024),
        name=kernel.__name__,
    )(*args)


def body(query, vision_kv, key_gain, out_grad, span_image, span_tiles):
    z, x, cores, tp = (lax.axis_size(name) for name in ("z", "x", "c", "tp"))
    own_rows = vision_kv.shape[0]
    column_rows = z * tp * own_rows
    image_rows = column_rows // 2
    members = x * cores

    def mesh_index():
        return lax.axis_index("z") * members, lax.axis_index("x") * cores + lax.axis_index("c"), cores

    mixed = jnp.sum(jnp.where(jnp.arange(span_image.shape[0]) % 2 == 1, span_image, -span_image)) > 0

    copies, normed, inverse = prepare(vision_kv, z)
    along_z = lax.all_to_all(copies, ("z", "tp"), split_axis=0, concat_axis=0, tiled=True)
    column = along_z.reshape(column_rows, 2 * HD)
    info, plane, gain = look(mesh_index, members, span_image, span_tiles, key_gain)

    def pass_on(blocks, step):
        count = z * members
        return lax.ppermute(blocks, ("z", "x", "c"), [(source, (source + step) % count) for source in range(count)])

    def travel(plane, gain, column):
        routed = small_call(route_kernel, (members, image_rows, 2 * HD), plane, gain, column)
        return lax.all_to_all(routed, ("c", "x"), split_axis=0, concat_axis=0, tiled=True)

    def travel_back(plane, terms):
        got = lax.all_to_all(terms, ("c", "x"), split_axis=0, concat_axis=0, tiled=True)
        return small_call(collect_kernel, column.shape, plane, got)

    def own_blocks(info, plane, gain, column, query, out_grad):
        attn_out, query_grad, terms = attention(info, query, out_grad, travel(plane, gain, column))
        return attn_out, query_grad, travel_back(plane, terms)

    def blocks_further(info, plane, gain, column, query, out_grad):
        come = pass_on(jnp.stack([query[:BLOCK], out_grad[:BLOCK]]), -1)
        attn_out, query_grad, back, terms = attention(info, query, out_grad, travel(plane, gain, column), come)
        home = pass_on(back, 1)
        terms = travel_back(plane, terms)
        outputs = [jnp.concatenate([home[k], rows[BLOCK:]], axis=0) for k, rows in enumerate((attn_out, query_grad))]
        return *outputs, terms

    attn_out, query_grad, terms = lax.cond(
        mixed, blocks_further, own_blocks, info, plane, gain, column, query, out_grad
    )
    got = lax.all_to_all(
        terms.reshape(z * tp, own_rows, 2 * HD), ("z", "tp"), split_axis=0, concat_axis=0, tiled=True
    )
    return (attn_out, query_grad, finish(got, normed, inverse, gain))


def solution(mesh):
    fine = Mesh(mesh.devices.reshape(8, 4, 2, 8), ("z", "x", "c", "tp"))
    seq = ("z", "x", "c")
    in_specs = (P(seq, "tp"), P(seq + ("tp",), None), P(), P(seq, "tp"), P(), P())
    out_specs = (P(seq, "tp"), P(seq, "tp"), P(seq + ("tp",), None))
    return jax.shard_map(body, mesh=fine, in_specs=in_specs, out_specs=out_specs, check_vma=False)
```

```python
import functools
import math

import jax
import jax.numpy as jnp
from jax import lax
from jax.experimental import pallas as pl
from jax.experimental.pallas import tpu as pltpu
from jax.sharding import Mesh, PartitionSpec as P

HD = 128
BLOCK = 64
TILES_IMG = 4

epsilon = 1e-05
neg_fill = -1e30
score_scale = 1.0 / math.sqrt(HD)

NN = (((1,), (0,)), ((), ()))
NT = (((1,), (1,)), ((), ()))
TN = (((0,), (0,)), ((), ()))


def dot(a, b, dims):
    return lax.dot_general(a, b, dims, preferred_element_type=jnp.float32)


def attention_kernel(further, info_ref, query_ref, grad_ref, *refs):
    come_ref = back_ref = None
    if further:
        come_ref, kv_ref, out_ref, query_grad_ref, back_ref, terms_ref, key_acc, value_acc = refs
    else:
        kv_ref, out_ref, query_grad_ref, terms_ref, key_acc, value_acc = refs
    groups, group_rows, _ = kv_ref.shape
    part = group_rows // TILES_IMG
    span = groups * group_rows
    heads = query_ref.shape[1] // HD
    lane = lax.broadcasted_iota(jnp.int32, info_ref.shape, 1)
    tiles = [jnp.sum(jnp.where(lane == k, info_ref[...], 0.0)).astype(jnp.int32) for k in range(2)]

    def keys():
        return kv_ref[:, :, :HD].reshape(span, HD)

    def values():
        return kv_ref[:, :, HD:].reshape(span, HD)

    def block_of(ref, other_ref, which, b):
        if further and b == 1:
            return other_ref.at[which]
        return ref.at[pl.ds((1 if further else b) * BLOCK, BLOCK)]

    def stacked(rows, first, count):
        return jnp.concatenate([rows[:, j * HD : (j + 1) * HD] for j in range(first, first + count)], axis=0)

    def unstack(rows, first, count, value):
        for j in range(count):
            rows[:, (first + j) * HD : (first + j + 1) * HD] = value[j * BLOCK : (j + 1) * BLOCK]

    per_chunk = 4
    column = lax.broadcasted_iota(jnp.int32, (1, span), 1)
    bias = [jnp.where((column & (group_rows - 1)) < n * part, 0.0, neg_fill) for n in tiles]
    live = [(n > 0).astype(jnp.float32) for n in tiles]

    def front(b, first):
        query = stacked(block_of(query_ref, come_ref, 0, b), first, per_chunk)
        grad = stacked(block_of(grad_ref, come_ref, 1, b), first, per_chunk)
        scores = dot(query, keys(), NT) + bias[b]
        prob_grad = dot(grad, values(), NT)
        return query, grad, scores, prob_grad

    def middle(b, first, query, grad, scores, prob_grad):
        row_max = jnp.max(scores, axis=1, keepdims=True)
        terms = jnp.exp2((scores - row_max) * (score_scale * math.log2(math.e)))
        inverse_sum = live[b] / jnp.sum(terms, axis=1, keepdims=True)
        weights = terms * inverse_sum
        probs = weights.astype(jnp.bfloat16)
        out = dot(probs, values(), NN).astype(jnp.bfloat16)
        unstack(block_of(out_ref, back_ref, 0, b), first, per_chunk, out)
        delta = jnp.sum(grad.astype(jnp.float32) * out.astype(jnp.float32), axis=1, keepdims=True)
        dscore = (weights * (prob_grad - delta)).astype(jnp.bfloat16)
        return probs, dscore

    def back(b, first, query, grad, probs, dscore):
        query_grad = (dot(dscore, keys(), NN) * score_scale).astype(jnp.bfloat16)
        unstack(block_of(query_grad_ref, back_ref, 1, b), first, per_chunk, query_grad)
        value_term = dot(probs, grad, TN)
        key_term = dot(dscore, query, TN)
        if (b, first) == chunks[0]:
            value_acc[...] = value_term
            key_acc[...] = key_term
        elif (b, first) == chunks[-1]:
            key_total = (key_acc[...] + key_term) * score_scale
            terms_ref[:, :, :HD] = key_total.astype(jnp.bfloat16).reshape(groups, group_rows, HD)
            terms_ref[:, :, HD:] = (value_acc[...] + value_term).astype(jnp.bfloat16).reshape(groups, group_rows, HD)
        else:
            value_acc[...] += value_term
            key_acc[...] += key_term

    chunks = [(b, first) for b in range(2) for first in range(0, heads, per_chunk)]
    held = None
    for chunk in chunks:
        query, grad, scores, prob_grad = front(*chunk)
        if held is not None:
            back(*held)
        probs, dscore = middle(*chunk, query, grad, scores, prob_grad)
        held = (*chunk, query, grad, probs, dscore)
    back(*held)


def attention(info, query, out_grad, kv, come=None):
    span = kv.shape[0] * kv.shape[1]
    vmem = pl.BlockSpec(memory_space=pltpu.VMEM)
    work = 6 * 2 * query.size * span
    moved = [] if come is None else [come]
    args = [info, query, out_grad, *moved, kv]
    shapes = [query.shape, query.shape, *(array.shape for array in moved), kv.shape]
    return pl.pallas_call(
        functools.partial(attention_kernel, come is not None),
        out_shape=[jax.ShapeDtypeStruct(shape, jnp.bfloat16) for shape in shapes],
        in_specs=[vmem] * len(args),
        out_specs=[vmem] * len(shapes),
        scratch_shapes=[pltpu.VMEM((span, HD), jnp.float32)] * 2,
        compiler_params=pltpu.CompilerParams(vmem_limit_bytes=40 * 1024 * 1024),
        cost_estimate=pl.CostEstimate(flops=work, bytes_accessed=5 * 1024 * 1024, transcendentals=query.size * span // HD),
        name="attention",
    )(*args)


def prepare_kernel(kv_ref, copies_ref, normed_ref, inverse_ref):
    heads = normed_ref.shape[1] // HD
    for t in range(heads):
        pre = kv_ref[:, 2 * t * HD : (2 * t + 1) * HD].astype(jnp.float32)
        inverse = lax.rsqrt(jnp.mean(pre * pre, axis=1, keepdims=True) + epsilon)
        normed_ref[:, t * HD : (t + 1) * HD] = pre * inverse
        inverse_ref[:, t * HD : (t + 1) * HD] = jnp.broadcast_to(inverse, pre.shape)
        for copy in range(t, copies_ref.shape[0], heads):
            copies_ref[copy] = kv_ref[:, 2 * t * HD : (2 * t + 2) * HD]


def prepare(vision_kv, copies):
    rows, columns = vision_kv.shape
    heads = columns // (2 * HD)
    vmem = pl.BlockSpec(memory_space=pltpu.VMEM)
    return pl.pallas_call(
        prepare_kernel,
        out_shape=[
            jax.ShapeDtypeStruct((copies * heads, rows, 2 * HD), jnp.bfloat16),
            jax.ShapeDtypeStruct((rows, heads * HD), jnp.float32),
            jax.ShapeDtypeStruct((rows, heads * HD), jnp.float32),
        ],
        in_specs=[vmem],
        out_specs=[vmem] * 3,
        compiler_params=pltpu.CompilerParams(vmem_limit_bytes=8 * 1024 * 1024),
        name="prepare",
    )(vision_kv)


def look_kernel(mesh_index, image_ref, tiles_ref, gain_ref, info_ref, plane_ref, kept_gain_ref):
    image, tiles = image_ref[...].astype(jnp.float32), tiles_ref[...].astype(jnp.float32)
    kept_gain_ref[...] = gain_ref[...]
    lane = lax.broadcasted_iota(jnp.int32, info_ref.shape, 1)
    plane, place, cores = mesh_index()
    begin = (plane + place) * 2
    blocks = image.shape[1]
    mixed = jnp.sum(jnp.where((lane & 1) == 1, image, -image), axis=1, keepdims=True)
    begin = begin + (mixed > 0.5).astype(jnp.int32)

    def entry(row, index):
        return jnp.sum(jnp.where(lane == (index & (blocks - 1)), row, 0.0), axis=1, keepdims=True)

    info_ref[...] = jnp.where(
        lane == 0, entry(tiles, begin), jnp.where(lane == 1, entry(tiles, begin + 1), jnp.where(lane == 2, mixed, 0.0))
    )
    members = plane_ref.shape[0]
    member = lax.broadcasted_iota(jnp.int32, (members, blocks), 0)
    member_lane = lax.broadcasted_iota(jnp.int32, (members, blocks), 1)
    first = plane * 2 + (mixed > 0.5).astype(jnp.int32)
    for core in range(cores):
        upper = member - core * (members // cores)
        first = first + jnp.where((upper >= 0) & (upper < members // cores), (upper * cores + core) * 2, 0)
    seen = jnp.sum(jnp.where(member_lane == first, image, 0.0), axis=1, keepdims=True)
    plane_ref[...] = jnp.broadcast_to(seen, plane_ref.shape)


def look(mesh_index, members, span_image, span_tiles, key_gain):
    vmem = pl.BlockSpec(memory_space=pltpu.VMEM)
    return pl.pallas_call(
        functools.partial(look_kernel, mesh_index),
        out_shape=[
            jax.ShapeDtypeStruct((1, HD), jnp.float32),
            jax.ShapeDtypeStruct((members, 2 * HD), jnp.float32),
            jax.ShapeDtypeStruct((1, HD), jnp.float32),
        ],
        in_specs=[vmem] * 3,
        out_specs=[vmem] * 3,
        compiler_params=pltpu.CompilerParams(vmem_limit_bytes=8 * 1024 * 1024),
        name="look",
    )(span_image.reshape(1, -1), span_tiles.reshape(1, -1), key_gain.reshape(1, -1))


def finish_kernel(got_ref, normed_ref, inverse_ref, gain_ref, out_ref):
    heads = out_ref.shape[1] // (2 * HD)
    gain = gain_ref[...]
    for t in range(heads):
        key_grad, value_grad = (
            sum(got_ref[k, :, part * HD : (part + 1) * HD].astype(jnp.float32) for k in range(t, got_ref.shape[0], heads))
            for part in range(2)
        )
        normed = normed_ref[:, t * HD : (t + 1) * HD]
        inverse = inverse_ref[:, t * HD : (t + 1) * HD]
        scaled = key_grad * gain
        pre_grad = inverse * (scaled - normed * jnp.mean(scaled * normed, axis=1, keepdims=True))
        out_ref[:, 2 * t * HD : (2 * t + 1) * HD] = pre_grad.astype(jnp.bfloat16)
        out_ref[:, (2 * t + 1) * HD : (2 * t + 2) * HD] = value_grad.astype(jnp.bfloat16)


def finish(got, normed, inverse, gain):
    rows = normed.shape[0]
    vmem = pl.BlockSpec(memory_space=pltpu.VMEM)
    return pl.pallas_call(
        finish_kernel,
        out_shape=jax.ShapeDtypeStruct((rows, 2 * normed.shape[1]), jnp.bfloat16),
        in_specs=[vmem] * 4,
        out_specs=vmem,
        compiler_params=pltpu.CompilerParams(vmem_limit_bytes=8 * 1024 * 1024),
        name="finish",
    )(got, normed, inverse, gain)


def route_kernel(plane_ref, gain_ref, column_ref, out_ref):
    members, image_rows, _ = out_ref.shape
    pre = column_ref[:, :HD].astype(jnp.float32)
    inverse = lax.rsqrt(jnp.mean(pre * pre, axis=1, keepdims=True) + epsilon)
    keys = (pre * inverse * gain_ref[...]).astype(jnp.bfloat16)
    for half, rows in enumerate((keys, column_ref[:, HD:])):
        part = slice(half * HD, (half + 1) * HD)
        for k in range(members):
            out_ref[k, :, part] = jnp.where(plane_ref[k : k + 1, part] > 0.5, rows[image_rows:], rows[:image_rows])


def collect_kernel(plane_ref, got_ref, out_ref):
    members, image_rows, _ = got_ref.shape
    totals = [0.0, 0.0]
    for k in range(members):
        term = got_ref[k].astype(jnp.float32)
        second = plane_ref[k : k + 1, :] > 0.5
        totals = [totals[0] + jnp.where(second, 0.0, term), totals[1] + jnp.where(second, term, 0.0)]
    for image in range(2):
        out_ref[image * image_rows : (image + 1) * image_rows, :] = totals[image].astype(jnp.bfloat16)


def small_call(kernel, shape, *args):
    vmem = pl.BlockSpec(memory_space=pltpu.VMEM)
    return pl.pallas_call(
        kernel,
        out_shape=jax.ShapeDtypeStruct(shape, jnp.bfloat16),
        in_specs=[vmem] * len(args),
        out_specs=vmem,
        compiler_params=pltpu.CompilerParams(vmem_limit_bytes=8 * 1024 * 1024),
        name=kernel.__name__,
    )(*args)


def body(query, vision_kv, key_gain, out_grad, span_image, span_tiles):
    z, x, cores, tp = (lax.axis_size(name) for name in ("z", "x", "c", "tp"))
    own_rows = vision_kv.shape[0]
    column_rows = z * tp * own_rows
    image_rows = column_rows // 2
    members = x * cores

    def mesh_index():
        return lax.axis_index("z") * members, lax.axis_index("x") * cores + lax.axis_index("c"), cores

    mixed = jnp.sum(jnp.where(jnp.arange(span_image.shape[0]) % 2 == 1, span_image, -span_image)) > 0

    copies, normed, inverse = prepare(vision_kv, z)
    along_z = lax.all_to_all(copies, ("z", "tp"), split_axis=0, concat_axis=0, tiled=True)
    column = along_z.reshape(column_rows, 2 * HD)
    info, plane, gain = look(mesh_index, members, span_image, span_tiles, key_gain)

    def pass_on(blocks, step):
        count = z * members
        return lax.ppermute(blocks, ("z", "x", "c"), [(source, (source + step) % count) for source in range(count)])

    def travel(plane, gain, column):
        routed = small_call(route_kernel, (members, image_rows, 2 * HD), plane, gain, column)
        return lax.all_to_all(routed, ("c", "x"), split_axis=0, concat_axis=0, tiled=True)

    def travel_back(plane, terms):
        got = lax.all_to_all(terms, ("c", "x"), split_axis=0, concat_axis=0, tiled=True)
        return small_call(collect_kernel, column.shape, plane, got)

    def own_blocks(info, plane, gain, column, query, out_grad):
        attn_out, query_grad, terms = attention(info, query, out_grad, travel(plane, gain, column))
        return attn_out, query_grad, travel_back(plane, terms)

    def blocks_further(info, plane, gain, column, query, out_grad):
        come = pass_on(jnp.stack([query[:BLOCK], out_grad[:BLOCK]]), -1)
        attn_out, query_grad, back, terms = attention(info, query, out_grad, travel(plane, gain, column), come)
        home = pass_on(back, 1)
        terms = travel_back(plane, terms)
        outputs = [jnp.concatenate([home[k], rows[BLOCK:]], axis=0) for k, rows in enumerate((attn_out, query_grad))]
        return *outputs, terms

    attn_out, query_grad, terms = lax.cond(
        mixed, blocks_further, own_blocks, info, plane, gain, column, query, out_grad
    )
    got = lax.all_to_all(
        terms.reshape(z * tp, own_rows, 2 * HD), ("z", "tp"), split_axis=0, concat_axis=0, tiled=True
    )
    return (attn_out, query_grad, finish(got, normed, inverse, gain))


def solution(mesh):
    fine = Mesh(mesh.devices.reshape(8, 4, 2, 8), ("z", "x", "c", "tp"))
    seq = ("z", "x", "c")
    in_specs = (P(seq, "tp"), P(seq + ("tp",), None), P(), P(seq, "tp"), P(), P())
    out_specs = (P(seq, "tp"), P(seq, "tp"), P(seq + ("tp",), None))
    return jax.shard_map(body, mesh=fine, in_specs=in_specs, out_specs=out_specs, check_vma=False)
```
